32 devices in a mesh: dp: 8 (over z, y), mp: 4 (over x, core).
Axes of the slice: x: 2, y: 2, z: 4, core: 2. Of those that a mesh axis runs over, the one named last changes fastest.
Arguments:
- frames: float32 [3584, 1536], P('dp', 'mp'), may hold values from -6 to 6
- norm_gain: float32 [1536], replicated, may hold values from 0.1 to 1.9
- w_in: float32 [1536, 6144], P(None, 'mp'), may hold values from -0.15625 to 0.15625
- w_out: float32 [6144, 1536], P('mp'), may hold values from -0.078125 to 0.078125
- head_weight: float32 [4, 1536, 1024], P('mp'), as said below
- teacher: int32 [4, 3584], P('mp', 'dp'), may hold values from 0 to 1023
Outputs:
- loss: float32 [], replicated
- grad_in: float32 [1536, 6144], P('dp', 'mp')
- grad_out: float32 [6144, 1536], P('mp', 'dp')
- grad_head: float32 [4, 1536, 1024], P('mp', 'dp')
The draws below stay inside these ranges and needn't reach their ends.
Inputs may be any that keep to these rules, and one draw needn't show every extreme that they name: `head_weight`: each head's projection has independent entries of order 1536 ** -0.5 times a per-code factor.
All inputs are finite; a program needn't handle non-finite values.
Results may differ from the reference program's by a relative error of at most 0.0003.
Values sent between devices are 32-bit elements; how exact they have to be, the bound alone decides.
A program may use at most 128 MiB of HBM per device.

```python
import jax
import jax.numpy as jnp
from jax import lax

D = 1536
FF = 6144
CODES = 1024
HEADS = 4
FRAMES = 3584


def draw_head_weight(key, part):
    base_key, scale_key = jax.random.split(jax.random.fold_in(key, 4177), 2)
    values = jax.random.normal(base_key, (HEADS, D, CODES), jnp.float32) * D ** (-0.5)
    factor = jnp.exp(jax.random.uniform(scale_key, (HEADS, 1, CODES), jnp.float32, -0.7, 0.7))
    return values * factor


def touch_ends(array, rng, least, largest):
    longest = array.shape.index(max(array.shape))
    spots = []
    for shift in (0, 1):
        where = [jax.random.randint(jax.random.fold_in(rng, axis), (), 0, length) for axis, length in enumerate(array.shape)]
        where[longest] = (where[longest] + shift) % array.shape[longest]
        spots.append(tuple(where))
    return array.at[spots[0]].set(least).at[spots[1]].set(largest)


def level_of(own_key, dims, pieces, smallest, top_value):
    def one(dim, blocks):
        heights = jax.random.uniform(jax.random.fold_in(jax.random.fold_in(own_key, 6), dim), (blocks,), jnp.float32, smallest / len(pieces), top_value / len(pieces))
        return jnp.repeat(jnp.exp(heights), dims[dim] // blocks).reshape((-1,) + (1,) * (len(dims) - dim - 1))

    factor_of = one(*pieces[0])
    for cut in pieces[1:]:
        factor_of = factor_of * one(*cut)
    return factor_of


def bell_draw(stream_key, dims, width, limit, pieces=(), held_as=jnp.bfloat16):
    factor_of = level_of(stream_key, dims, pieces, -0.22, 0.18) if pieces else 1.0
    values = jax.random.normal(stream_key, dims, jnp.float32) * width * factor_of
    return jnp.minimum(jnp.maximum(values, -limit), limit).astype(held_as)


def setup_inputs(seed: int = 0) -> dict:
    seeds = jax.random.split(jax.random.key(seed), 7)
    return {
        "frames": bell_draw(seeds[0], (FRAMES, D), 1.0, 6.0, ((0, 8), (1, 4)), jnp.float32),
        "norm_gain": jnp.clip(1.0 + 0.18 * jax.random.normal(seeds[1], (D,), jnp.float32), 0.1, 1.9),
        "w_in": bell_draw(seeds[2], (D, FF), D ** -0.5, 0.15625, ((1, 4),), jnp.float32),
        "w_out": bell_draw(seeds[3], (FF, D), FF ** -0.5, 0.078125, ((0, 4),), jnp.float32),
        "head_weight": draw_head_weight(jax.random.fold_in(seeds[6], 71), 0),
        "teacher": touch_ends(jax.random.randint(seeds[5], (HEADS, FRAMES), 0, CODES), jax.random.fold_in(seeds[5], 1), 0, CODES - 1).astype(jnp.int32),
    }


HI = lax.Precision.HIGHEST

def reference(frames, norm_gain, w_in, w_out, head_weight, teacher):
    mean = lax.optimization_barrier(jnp.mean(frames, axis=1, keepdims=True))
    centred = frames - mean
    var = lax.optimization_barrier(jnp.mean(centred * centred, axis=1, keepdims=True))
    normed = centred * lax.rsqrt(var + 1e-05) * norm_gain
    pre = jnp.dot(normed, w_in, precision=HI)
    sig = jax.nn.sigmoid(pre)
    act = pre * sig
    mixed = frames + 0.5 * jnp.dot(act, w_out, precision=HI)
    codes = jnp.arange(head_weight.shape[2], dtype=jnp.int32)

    def one_head(carry, item):
        weight, target = item
        logits = jnp.dot(mixed, weight, precision=HI)
        top = lax.optimization_barrier(jnp.max(logits, axis=1, keepdims=True))
        expo = jnp.exp(logits - top)
        total = lax.optimization_barrier(jnp.sum(expo, axis=1, keepdims=True))
        lse = top + jnp.log(total)
        onehot = (target[:, None] == codes[None, :]).astype(jnp.float32)
        picked = lax.optimization_barrier(jnp.sum(logits * onehot, axis=1, keepdims=True))
        dlogits = expo / total - onehot
        grad = jnp.dot(mixed.T, dlogits, precision=HI)
        loss_acc, dmix = carry
        dmix = dmix + jnp.dot(dlogits, weight.T, precision=HI)
        loss_acc = loss_acc + jnp.sum(lse - picked)
        return ((loss_acc, dmix), grad)
    start = (jnp.zeros((), jnp.float32), jnp.zeros_like(mixed))
    (loss_total, dmixed), grad_head = lax.scan(one_head, start, (head_weight, teacher))
    dffn = 0.5 * dmixed
    grad_out = jnp.dot(act.T, dffn, precision=HI)
    dact = jnp.dot(dffn, w_out.T, precision=HI)
    dpre = dact * sig * (1.0 + pre * (1.0 - sig))
    grad_in = jnp.dot(normed.T, dpre, precision=HI)
    loss = loss_total / (FRAMES * HEADS)
    return (loss, grad_in, grad_out, grad_head)
```

```python
import jax
import jax.numpy as jnp
from jax import lax
from jax.sharding import PartitionSpec as P

HI = lax.Precision.HIGH
PARTS = 2


def mm(a, b):
    return jnp.dot(a, b, precision=HI, preferred_element_type=jnp.float32)


def mm_t(a, b):
    return lax.dot_general(a, b, (((0,), (0,)), ((), ())), precision=HI, preferred_element_type=jnp.float32)


def mm_nt(a, b):
    return lax.dot_general(a, b, (((1,), (1,)), ((), ())), precision=HI, preferred_element_type=jnp.float32)


def swap(x, axis, size, bit):
    return lax.ppermute(x, axis, [(i, i ^ bit) for i in range(size)])


def bits_of(size):
    bits, bit = [], 1
    while bit < size:
        bits.append(bit)
        bit *= 2
    return bits


def gather_columns(x, axis, size):
    me = lax.axis_index(axis)
    for bit in reversed(bits_of(size)):
        other = swap(x, axis, size, bit)
        x = jnp.concatenate([x[None], other[None]], axis=0) if bit == bits_of(size)[-1] else jnp.concatenate([x, other], axis=0)
    codes = [0]
    for bit in reversed(bits_of(size)):
        codes = codes + [c ^ bit for c in codes]
    place = {c: k for k, c in enumerate(codes)}
    slots = jnp.asarray([place[c] for c in range(size)], jnp.int32)
    picked = [lax.dynamic_index_in_dim(x, slots[me ^ d], 0, keepdims=False) for d in range(size)]
    return jnp.concatenate(picked, axis=1)


def scatter_rows(x, axis, size):
    me = lax.axis_index(axis)
    for bit in bits_of(size):
        half = x.shape[0] // 2
        up = (me // bit) % 2
        mine = lax.dynamic_slice_in_dim(x, up * half, half, 0)
        theirs = lax.dynamic_slice_in_dim(x, (1 - up) * half, half, 0)
        x = mine + swap(theirs, axis, size, bit)
    return x


def own_rows(x, axis, size):
    me = lax.axis_index(axis)
    start = 0
    rows = x.shape[0]
    for bit in bits_of(size):
        rows = rows // 2
        start = start + ((me // bit) % 2) * rows
    return lax.dynamic_slice_in_dim(x, start, rows, 0)


def gather_rows(x, axis, size):
    me = lax.axis_index(axis)
    for bit in reversed(bits_of(size)):
        other = swap(x, axis, size, bit)
        up = (me // bit) % 2
        first = jnp.where(up == 0, x, other)
        second = jnp.where(up == 0, other, x)
        x = jnp.concatenate([first, second], axis=0)
    return x


def sum_scalar(x, axis, size):
    for bit in bits_of(size):
        x = x + swap(x, axis, size, bit)
    return x


def ring_order(size):
    b = 1
    for c in bits_of(size):
        if c * c <= size and size % c == 0:
            b = c
    a = size // b
    if b == 1:
        return list(range(size))
    order = [r * b for r in range(a)]
    for k, r in enumerate(reversed(range(a))):
        cols = list(range(1, b))
        order += [r * b + c for c in (cols if k % 2 == 0 else cols[::-1])]
    return order


def ring_scatter(x, axis, size):
    order = ring_order(size)
    rank = [0] * size
    for p, d in enumerate(order):
        rank[d] = p
    me = lax.axis_index(axis)
    pos = jnp.asarray(rank, jnp.int32)[me]
    table = jnp.asarray(order, jnp.int32)
    block = x.shape[0] // size
    half = block // 2

    def part(q, side):
        owner = table[lax.rem(q + 2 * size, size)]
        return lax.dynamic_slice_in_dim(x, owner * block + side * half, half, 0)

    right = [(order[p], order[(p + 1) % size]) for p in range(size)]
    left = [(order[p], order[(p - 1) % size]) for p in range(size)]
    a = part(pos - 1, 0)
    b = part(pos + 1, 1)
    for s in range(size - 1):
        a = lax.ppermute(a, axis, right) + part(pos - s - 2, 0)
        b = lax.ppermute(b, axis, left) + part(pos + s + 2, 1)
    return jnp.concatenate([a, b], axis=0)


def make_body(n_dp, n_mp):
    def body(frames, norm_gain, w_in, w_out, head_weight, teacher):
        whole = gather_columns(frames, "mp", n_mp)
        rows = whole.shape[0]
        cut = rows // PARTS
        weight = head_weight[0]
        target = teacher[0]
        codes = jnp.arange(weight.shape[1], dtype=jnp.int32)
        normed, pre, sig, act, mixed = [], [], [], [], []
        for k in range(PARTS):
            x = whole[k * cut:(k + 1) * cut]
            mean = jnp.mean(x, axis=1, keepdims=True)
            centred = x - mean
            var = jnp.mean(centred * centred, axis=1, keepdims=True)
            normed.append(centred * lax.rsqrt(var + 1e-05) * norm_gain)
            pre.append(mm(normed[k], w_in))
            sig.append(jax.nn.sigmoid(pre[k]))
            act.append(pre[k] * sig[k])
            summed = scatter_rows(mm(act[k], w_out), "mp", n_mp)
            mixed.append(gather_rows(own_rows(x, "mp", n_mp) + 0.5 * summed, "mp", n_mp))
        dlogits, dffn, local_loss = [], [], 0.0
        for k in range(PARTS):
            logits = mm(mixed[k], weight)
            top = jnp.max(logits, axis=1, keepdims=True)
            expo = jnp.exp(logits - top)
            total = jnp.sum(expo, axis=1, keepdims=True)
            lse = top + jnp.log(total)
            onehot = (target[k * cut:(k + 1) * cut, None] == codes[None, :]).astype(jnp.float32)
            picked = jnp.sum(logits * onehot, axis=1, keepdims=True)
            dlogits.append(expo / total - onehot)
            local_loss = local_loss + jnp.sum(lse - picked)
            dpartial = mm_nt(dlogits[k], weight)
            dffn.append(gather_rows(0.5 * scatter_rows(dpartial, "mp", n_mp), "mp", n_mp))
        cat = lambda v: jnp.concatenate(v, axis=0)
        grad_head = ring_scatter(mm_t(cat(mixed), cat(dlogits)), "dp", n_dp)
        dffn = cat(dffn)
        grad_out = ring_scatter(mm_t(dffn, cat(act)), "dp", n_dp)
        pre, sig = cat(pre), cat(sig)
        dpre = mm_nt(dffn, w_out) * sig * (1.0 + pre * (1.0 - sig))
        grad_in = ring_scatter(mm_t(cat(normed), dpre), "dp", n_dp)
        loss_total = sum_scalar(sum_scalar(local_loss, "mp", n_mp), "dp", n_dp)
        loss = loss_total / (rows * n_dp * head_weight.shape[0] * n_mp)
        return (loss, grad_in, grad_out.T, grad_head[None])

    return body


def solution(mesh):
    placed = (P("dp", "mp"), P(), P(None, "mp"), P("mp", None), P("mp", None, None), P("mp", "dp"))
    return jax.shard_map(
        make_body(mesh.shape["dp"], mesh.shape["mp"]),
        mesh=mesh,
        in_specs=placed,
        out_specs=(P(), P("dp", "mp"), P("mp", "dp"), P("mp", "dp", None)),
        check_vma=False,
    )
```

```python
import jax
import jax.numpy as jnp
from jax import lax
from jax.sharding import PartitionSpec as P

HI = lax.Precision.HIGH
PARTS = 2


def mm(a, b):
    return jnp.dot(a, b, precision=HI, preferred_element_type=jnp.float32)


def mm_t(a, b):
    return lax.dot_general(a, b, (((0,), (0,)), ((), ())), precision=HI, preferred_element_type=jnp.float32)


def mm_nt(a, b):
    return lax.dot_general(a, b, (((1,), (1,)), ((), ())), precision=HI, preferred_element_type=jnp.float32)


def swap(x, axis, size, bit):
    return lax.ppermute(x, axis, [(i, i ^ bit) for i in range(size)])


def bits_of(size):
    bits, bit = [], 1
    while bit < size:
        bits.append(bit)
        bit *= 2
    return bits


def gather_columns(x, axis, size):
    me = lax.axis_index(axis)
    pieces = {0: x}
    for bit in reversed(bits_of(size)):
        pieces.update({c ^ bit: swap(v, axis, size, bit) for c, v in list(pieces.items())})
    for bit in bits_of(size):
        up = (me & bit) != 0
        pieces = {c: jnp.where(up, pieces[c ^ bit], v) for c, v in pieces.items()}
    return jnp.concatenate([pieces[d] for d in range(size)], axis=1)


def halve(x, axis, size, bit):
    me = lax.axis_index(axis)
    half = x.shape[0] // 2
    up = (me // bit) % 2
    mine = lax.dynamic_slice_in_dim(x, up * half, half, 0)
    theirs = lax.dynamic_slice_in_dim(x, (1 - up) * half, half, 0)
    return mine + swap(theirs, axis, size, bit)


def scatter_rows(x, axis, size, bits):
    for bit in bits:
        x = halve(x, axis, size, bit)
    return x


def own_rows(x, axis, size):
    me = lax.axis_index(axis)
    start = 0
    rows = x.shape[0]
    for bit in bits_of(size):
        rows = rows // 2
        start = start + ((me // bit) % 2) * rows
    return lax.dynamic_slice_in_dim(x, start, rows, 0)


def gather_rows(x, axis, size):
    me = lax.axis_index(axis)
    for bit in reversed(bits_of(size)):
        other = swap(x, axis, size, bit)
        up = (me // bit) % 2
        first = jnp.where(up == 0, x, other)
        second = jnp.where(up == 0, other, x)
        x = jnp.concatenate([first, second], axis=0)
    return x


def tie(x, *rings):
    held = lax.optimization_barrier((x,) + tuple((r.a, r.b) for r in rings))
    for r, (a, b) in zip(rings, held[1:]):
        r.a, r.b = a, b
    return held[0]


def ring_order(size):
    b = 1
    for c in bits_of(size):
        if c * c <= size and size % c == 0:
            b = c
    a = size // b
    if b == 1:
        return list(range(size))
    order = [r * b for r in range(a)]
    for k, r in enumerate(reversed(range(a))):
        cols = list(range(1, b))
        order += [r * b + c for c in (cols if k % 2 == 0 else cols[::-1])]
    return order


class Ring:
    def __init__(self, x, axis, size):
        self.x, self.axis, self.size, self.done = x, axis, size, 0
        self.order = ring_order(size)
        rank = [0] * size
        for p, d in enumerate(self.order):
            rank[d] = p
        self.pos = jnp.asarray(rank, jnp.int32)[lax.axis_index(axis)]
        self.table = jnp.asarray(self.order, jnp.int32)
        self.half = x.shape[0] // size // 2
        self.a = self.part(self.pos - 1, 0)
        self.b = self.part(self.pos + 1, 1)

    def part(self, q, side):
        owner = self.table[lax.rem(q + 2 * self.size, self.size)]
        return lax.dynamic_slice_in_dim(self.x, (2 * owner + side) * self.half, self.half, 0)

    def step(self):
        if self.done < self.size - 1:
            o, n, s = self.order, self.size, self.done
            right = [(o[p], o[(p + 1) % n]) for p in range(n)]
            left = [(o[p], o[(p - 1) % n]) for p in range(n)]
            self.a = lax.ppermute(self.a, self.axis, right) + self.part(self.pos - s - 2, 0)
            self.b = lax.ppermute(self.b, self.axis, left) + self.part(self.pos + s + 2, 1)
            self.done = s + 1

    def result(self):
        while self.done < self.size - 1:
            self.step()
        return jnp.concatenate([self.a, self.b], axis=0)


def make_body(n_dp, n_mp):
    bits = bits_of(n_mp)

    def body(frames, norm_gain, w_in, w_out, head_weight, teacher):
        whole = gather_columns(frames, "mp", n_mp)
        rows = whole.shape[0]
        cut = rows // PARTS
        weight = head_weight[0]
        target = teacher[0]
        codes = jnp.arange(weight.shape[1], dtype=jnp.int32)
        normed, pre, sig, act, value, mixed = [], [], [], [], [], []
        for k in range(PARTS):
            x = whole[k * cut:(k + 1) * cut]
            mean = jnp.mean(x, axis=1, keepdims=True)
            centred = x - mean
            var = jnp.mean(centred * centred, axis=1, keepdims=True)
            normed.append(centred * lax.rsqrt(var + 1e-05) * norm_gain)
            pre.append(mm(normed[k], w_in))
            sig.append(jax.nn.sigmoid(pre[k]))
            act.append(pre[k] * sig[k])
            lhs = act[k]
            if k:
                lhs, value[k - 1] = lax.optimization_barrier((lhs, value[k - 1]))
            product = mm(lhs, w_out)
            if k:
                value[k - 1] = scatter_rows(value[k - 1], "mp", n_mp, bits[1:])
                product, value[k - 1] = lax.optimization_barrier((product, value[k - 1]))
            value.append(scatter_rows(product, "mp", n_mp, bits[:1]))
        value[-1] = scatter_rows(value[-1], "mp", n_mp, bits[1:])
        for k in range(PARTS):
            x = whole[k * cut:(k + 1) * cut]
            mixed.append(gather_rows(own_rows(x, "mp", n_mp) + 0.5 * value[k], "mp", n_mp))
        dlogits, local_loss = [], 0.0
        for k in range(PARTS):
            logits = mm(mixed[k], weight)
            top = jnp.max(logits, axis=1, keepdims=True)
            expo = jnp.exp(logits - top)
            total = jnp.sum(expo, axis=1, keepdims=True)
            lse = top + jnp.log(total)
            onehot = (target[k * cut:(k + 1) * cut, None] == codes[None, :]).astype(jnp.float32)
            picked = jnp.sum(logits * onehot, axis=1, keepdims=True)
            dlogits.append(expo / total - onehot)
            local_loss = local_loss + jnp.sum(lse - picked)
        cat = lambda v: jnp.concatenate(v, axis=0)
        dlogits = cat(dlogits)
        head = Ring(mm_t(cat(mixed), dlogits), "dp", n_dp)
        dlogits = tie(dlogits, head)
        head.step()
        dpartial = scatter_rows(mm_nt(dlogits, weight), "mp", n_mp, bits[:1])
        dpartial = tie(dpartial, head)
        head.step()
        dsum = 0.5 * scatter_rows(dpartial, "mp", n_mp, bits[1:])
        dsum = tie(dsum, head)
        head.step()
        dffn = gather_rows(dsum, "mp", n_mp)
        dffn = tie(dffn, head)
        head.step()
        out = Ring(mm_t(dffn, cat(act)), "dp", n_dp)
        pre, sig = cat(pre), cat(sig)
        dffn = tie(dffn, head, out)
        head.step()
        out.step()
        dpre = mm_nt(dffn, w_out) * sig * (1.0 + pre * (1.0 - sig))
        dpre = tie(dpre, head, out)
        head.step()
        out.step()
        into = Ring(mm_t(cat(normed), dpre), "dp", n_dp)
        head.step()
        loss = local_loss
        hops = [("mp", n_mp, bit) for bit in bits] + [("dp", n_dp, bit) for bit in bits_of(n_dp)]
        while into.done < n_dp - 1:
            for ring in (into, out, head):
                ring.step()
            if hops and into.done < n_dp - 1:
                loss = tie(loss, into)
                axis, size, bit = hops.pop(0)
                loss = loss + swap(loss, axis, size, bit)
        for axis, size, bit in hops:
            loss = loss + swap(loss, axis, size, bit)
        loss = loss / (rows * n_dp * head_weight.shape[0] * n_mp)
        return (loss, into.result(), out.result().T, head.result()[None])

    return body


def solution(mesh):
    placed = (P("dp", "mp"), P(), P(None, "mp"), P("mp", None), P("mp", None, None), P("mp", "dp"))
    return jax.shard_map(
        make_body(mesh.shape["dp"], mesh.shape["mp"]),
        mesh=mesh,
        in_specs=placed,
        out_specs=(P(), P("dp", "mp"), P("mp", "dp"), P("mp", "dp", None)),
        check_vma=False,
    )
```

```python
import jax
import jax.numpy as jnp
from jax import lax
from jax.sharding import PartitionSpec as P

HI = lax.Precision.HIGH
PARTS = 2


def mm(a, b):
    return jnp.dot(a, b, precision=HI, preferred_element_type=jnp.float32)


def mm_t(a, b):
    return lax.dot_general(a, b, (((0,), (0,)), ((), ())), precision=HI, preferred_element_type=jnp.float32)


def mm_nt(a, b):
    return lax.dot_general(a, b, (((1,), (1,)), ((), ())), precision=HI, preferred_element_type=jnp.float32)


def swap(x, axis, size, bit):
    return lax.ppermute(x, axis, [(i, i ^ bit) for i in range(size)])


def bits_of(size):
    bits, bit = [], 1
    while bit < size:
        bits.append(bit)
        bit *= 2
    return bits


def gather_columns(x, axis, size):
    me = lax.axis_index(axis)
    pieces = {0: x}
    for bit in reversed(bits_of(size)):
        pieces.update({c ^ bit: swap(v, axis, size, bit) for c, v in list(pieces.items())})
    for bit in bits_of(size):
        up = (me & bit) != 0
        pieces = {c: jnp.where(up, pieces[c ^ bit], v) for c, v in pieces.items()}
    return jnp.concatenate([pieces[d] for d in range(size)], axis=1)


def halve(x, axis, size, bit):
    me = lax.axis_index(axis)
    half = x.shape[0] // 2
    up = (me // bit) % 2
    mine = lax.dynamic_slice_in_dim(x, up * half, half, 0)
    theirs = lax.dynamic_slice_in_dim(x, (1 - up) * half, half, 0)
    return mine + swap(theirs, axis, size, bit)


def scatter_rows(x, axis, size, bits):
    for bit in bits:
        x = halve(x, axis, size, bit)
    return x


def own_rows(x, axis, size):
    me = lax.axis_index(axis)
    start = 0
    rows = x.shape[0]
    for bit in bits_of(size):
        rows = rows // 2
        start = start + ((me // bit) % 2) * rows
    return lax.dynamic_slice_in_dim(x, start, rows, 0)


def gather_rows(x, axis, size, bits):
    me = lax.axis_index(axis)
    for bit in reversed(bits):
        other = swap(x, axis, size, bit)
        up = (me // bit) % 2
        first = jnp.where(up == 0, x, other)
        second = jnp.where(up == 0, other, x)
        x = jnp.concatenate([first, second], axis=0)
    return x


def tie(x, *rings):
    held = lax.optimization_barrier((x,) + tuple((r.a, r.b) for r in rings))
    for r, (a, b) in zip(rings, held[1:]):
        r.a, r.b = a, b
    return held[0]


def ring_order(size):
    b = 1
    for c in bits_of(size):
        if c * c <= size and size % c == 0:
            b = c
    a = size // b
    if b == 1:
        return list(range(size))
    order = [r * b for r in range(a)]
    for k, r in enumerate(reversed(range(a))):
        cols = list(range(1, b))
        order += [r * b + c for c in (cols if k % 2 == 0 else cols[::-1])]
    return order


class Ring:
    def __init__(self, x, axis, size, extra=None):
        self.x, self.axis, self.size, self.done = x, axis, size, 0
        self.extra = extra
        self.order = ring_order(size)
        rank = [0] * size
        for p, d in enumerate(self.order):
            rank[d] = p
        self.pos = jnp.asarray(rank, jnp.int32)[lax.axis_index(axis)]
        self.table = jnp.asarray(self.order, jnp.int32)
        self.half = x.shape[0] // size // 2
        self.a = self.part(self.pos - 1, 0)
        self.b = self.part(self.pos + 1, 1)

    def part(self, q, side):
        owner = self.table[lax.rem(q + 2 * self.size, self.size)]
        rows = lax.dynamic_slice_in_dim(self.x, (2 * owner + side) * self.half, self.half, 0)
        if side == 0 and self.extra is not None:
            rows = jnp.concatenate([rows, self.extra], axis=0)
        return rows

    def step(self):
        if self.done < self.size - 1:
            o, n, s = self.order, self.size, self.done
            right = [(o[p], o[(p + 1) % n]) for p in range(n)]
            left = [(o[p], o[(p - 1) % n]) for p in range(n)]
            self.a = lax.ppermute(self.a, self.axis, right) + self.part(self.pos - s - 2, 0)
            self.b = lax.ppermute(self.b, self.axis, left) + self.part(self.pos + s + 2, 1)
            self.done = s + 1

    def result(self):
        while self.done < self.size - 1:
            self.step()
        return jnp.concatenate([self.a[:self.half], self.b], axis=0)


def make_body(n_dp, n_mp):
    bits = bits_of(n_mp)

    def body(frames, norm_gain, w_in, w_out, head_weight, teacher):
        whole = gather_columns(frames, "mp", n_mp)
        rows = whole.shape[0]
        cut = rows // PARTS
        weight = head_weight[0]
        target = teacher[0]
        codes = jnp.arange(weight.shape[1], dtype=jnp.int32)
        normed, pre, sig, act, value, mixed = [], [], [], [], [], []
        for k in range(PARTS):
            x = whole[k * cut:(k + 1) * cut]
            mean = jnp.mean(x, axis=1, keepdims=True)
            centred = x - mean
            var = jnp.mean(centred * centred, axis=1, keepdims=True)
            normed.append(centred * lax.rsqrt(var + 1e-05) * norm_gain)
            pre.append(mm(normed[k], w_in))
            sig.append(jax.nn.sigmoid(pre[k]))
            act.append(pre[k] * sig[k])
            lhs = act[k]
            if k:
                lhs, value[k - 1] = lax.optimization_barrier((lhs, value[k - 1]))
            product = mm(lhs, w_out)
            if k:
                value[k - 1] = scatter_rows(value[k - 1], "mp", n_mp, bits[1:])
                product, value[k - 1] = lax.optimization_barrier((product, value[k - 1]))
            value.append(scatter_rows(product, "mp", n_mp, bits[:1]))
        for k in range(PARTS):
            x = own_rows(whole[k * cut:(k + 1) * cut], "mp", n_mp)
            if k:
                value[k] = scatter_rows(value[k], "mp", n_mp, bits[1:])
                value[k], mixed[k - 1] = lax.optimization_barrier((value[k], mixed[k - 1]))
                mixed[k - 1] = gather_rows(mixed[k - 1], "mp", n_mp, bits[:1])
            mixed.append(gather_rows(x + 0.5 * value[k], "mp", n_mp, bits[1:]))
        mixed[-1] = gather_rows(mixed[-1], "mp", n_mp, bits[:1])
        dlogits, local_loss = [], 0.0
        for k in range(PARTS):
            logits = mm(mixed[k], weight)
            top = jnp.max(logits, axis=1, keepdims=True)
            expo = jnp.exp(logits - top)
            total = jnp.sum(expo, axis=1, keepdims=True)
            lse = top + jnp.log(total)
            onehot = (target[k * cut:(k + 1) * cut, None] == codes[None, :]).astype(jnp.float32)
            picked = jnp.sum(logits * onehot, axis=1, keepdims=True)
            dlogits.append(expo / total - onehot)
            local_loss = local_loss + jnp.sum(lse - picked)
        cat = lambda v: jnp.concatenate(v, axis=0)
        dlogits = cat(dlogits)
        extra = jnp.broadcast_to(local_loss, (8, dlogits.shape[1]))
        head = Ring(mm_t(cat(mixed), dlogits), "dp", n_dp, extra)
        dlogits = tie(dlogits, head)
        head.step()
        dpartial = scatter_rows(mm_nt(dlogits, weight), "mp", n_mp, bits[:1])
        dsum = 0.5 * scatter_rows(dpartial, "mp", n_mp, bits[1:])
        dsum = tie(dsum, head)
        head.step()
        dffn = gather_rows(dsum, "mp", n_mp, bits[1:])
        dffn = tie(dffn, head)
        head.step()
        dffn = gather_rows(dffn, "mp", n_mp, bits[:1])
        out = Ring(mm_t(dffn, cat(act)), "dp", n_dp)
        pre, sig = cat(pre), cat(sig)
        dffn = tie(dffn, head, out)
        head.step()
        out.step()
        dpre = mm_nt(dffn, w_out) * sig * (1.0 + pre * (1.0 - sig))
        dpre = tie(dpre, head, out)
        head.step()
        out.step()
        into = Ring(mm_t(cat(normed), dpre), "dp", n_dp)
        head.step()
        while into.done < n_dp - 1:
            for ring in (head, into, out):
                ring.step()
            if head.done < n_dp - 1:
                into.a = tie(into.a, head)
        loss = head.a[head.half, 0]
        for bit in bits:
            loss = loss + swap(loss, "mp", n_mp, bit)
        loss = loss / (rows * n_dp * head_weight.shape[0] * n_mp)
        return (loss, into.result(), out.result().T, head.result()[None])

    return body


def solution(mesh):
    placed = (P("dp", "mp"), P(), P(None, "mp"), P("mp", None), P("mp", None, None), P("mp", "dp"))
    return jax.shard_map(
        make_body(mesh.shape["dp"], mesh.shape["mp"]),
        mesh=mesh,
        in_specs=placed,
        out_specs=(P(), P("dp", "mp"), P("mp", "dp"), P("mp", "dp", None)),
        check_vma=False,
    )
```
